256 devices in a mesh: subj: 16 (over z_lo, x, core), space: 16 (over z_hi, y).
Axes of the slice: x: 4, y: 4, z: 8 (z_hi: 4, z_lo: 2; z = z_hi * 2 + z_lo), core: 2. Of those that a mesh axis runs over, the one named last changes fastest.
Arguments:
- image: bfloat16 [32, 16, 24, 48, 128], P('subj', 'space'), may hold values from -6 to 6
- momentum: bfloat16 [32, 3, 16, 24, 48, 128], P('subj', None, 'space'), may hold values from -128 to 128
- tissue_flags: int32 [32, 16], P('subj', 'space'), may hold values 0 or 1
- band_widths: int32 [3], replicated, may hold values from 8 to 12, as said below
Outputs:
- mismatch: bfloat16 [32, 16, 24, 48, 128], P('subj', 'space')
- template: float32 [16, 24, 48, 128], P('space')
The draws below stay inside these ranges and needn't reach their ends.
Inputs may be any that keep to these rules, and one draw needn't show every extreme that they name: `band_widths`: the three widths are 8, 10 and 12 in some order.
All inputs are finite; a program needn't handle non-finite values. No bound on the sum of `tissue_flags` on one device may be relied on, other than what follows from the above.
Results may differ from the reference program's by a relative error of at most 0.001.
Values sent between devices are 32-bit elements; how exact they have to be, the bound alone decides.
A program may use at most 64 MiB of HBM per device.

```python
import jax
import jax.numpy as jnp
from jax import lax

CX = 24
CY = 48
CZ = 128
TGY = 4
HALO = 12
STEPS = 4
SUBJECTS = 32
TILES = 16
N_SPACE = 16


def draw_band_widths(key, part):
    key = jax.random.fold_in(key, 7)
    order = jax.random.permutation(key, 3).astype(jnp.int32)
    return (HALO - 4 + 2 * order).astype(jnp.int32)


def place_ends(drawn, own_key, least, largest):
    extent = drawn.shape
    place = [jax.random.randint(jax.random.fold_in(own_key, axis), (), 0, extent[axis]) for axis in range(len(extent))]
    drawn = drawn.at[tuple(place)].set(least)
    longest = extent.index(max(extent))
    place[longest] = (place[longest] + 1) % extent[longest]
    return drawn.at[tuple(place)].set(largest)


def block_levels(own_key, dims, split, smallest, top_value):
    gain, own = 1.0, jax.random.fold_in(own_key, 6)
    for axis_at, blocks in split:
        draws = jnp.exp(jax.random.uniform(jax.random.fold_in(own, axis_at), (blocks,), jnp.float32, smallest / len(split), top_value / len(split)))
        gain = gain * jnp.repeat(draws, dims[axis_at] // blocks).reshape([-1 if axis == axis_at else 1 for axis in range(len(dims))])
    return gain


def scatter_about(own_key, extent, scale, most, pieces=(), dtype=jnp.bfloat16):
    entries = jax.random.normal(own_key, extent, jnp.float32) * scale
    if len(pieces) > 0:
        entries = block_levels(own_key, extent, pieces, -0.22, 0.18) * entries
    return jnp.clip(entries, min=-most, max=most).astype(dtype)


def setup_inputs(seed: int = 0) -> dict:
    key_of = jax.random.split(jax.random.key(seed), 5)
    return {
        "image": scatter_about(key_of[0], (SUBJECTS, TILES, CX, CY, CZ), 1.0, 6.0, ((0, 16), (1, 16))),
        "momentum": scatter_about(key_of[1], (SUBJECTS, 3, TILES, CX, CY, CZ), 24.0, 128.0, ((0, 16), (2, 16))),
        "tissue_flags": place_ends((jax.random.randint(key_of[2], (SUBJECTS, TILES), 0, 4) < 3).astype(jnp.int32), jax.random.fold_in(key_of[2], 1), 0, 1),
        "band_widths": draw_band_widths(jax.random.fold_in(key_of[4], 71), 0),
    }


def assemble(tiles):
    lead = tiles.shape[:-4]
    grid_rows = N_SPACE // TGY
    shaped = tiles.reshape(lead + (grid_rows, TGY, CX, CY, CZ))
    shaped = jnp.swapaxes(shaped, -4, -3)
    return shaped.reshape(lead + (grid_rows * CX, TGY * CY, CZ))


def split_tiles(volume):
    lead = volume.shape[:-3]
    grid_rows = N_SPACE // TGY
    shaped = volume.reshape(lead + (grid_rows, CX, TGY, CY, CZ))
    shaped = jnp.swapaxes(shaped, -4, -3)
    return shaped.reshape(lead + (N_SPACE, CX, CY, CZ))


def smooth_axis(field, width, axis):
    count = field.shape[axis]
    pads = [(0, 0)] * field.ndim
    pads[axis] = (HALO, HALO)
    padded = jnp.pad(field, pads)
    total = jnp.zeros_like(field)
    for offset in range(-HALO, HALO + 1):
        dist = jnp.float32(abs(offset))
        coeff = jnp.where(dist <= width, (width + 1.0 - dist) / ((width + 1.0) * (width + 1.0)), 0.0)
        total = total + coeff * lax.slice_in_dim(padded, HALO + offset, HALO + offset + count, axis=axis)
    return total


def neighbours(field, axis):
    pads = [(0, 0)] * field.ndim
    pads[axis] = (1, 1)
    padded = jnp.pad(field, pads)
    count = field.shape[axis]
    lower = lax.slice_in_dim(padded, 0, count, axis=axis)
    upper = lax.slice_in_dim(padded, 2, count + 2, axis=axis)
    return lower, upper


def reference(image, momentum, tissue_flags, band_widths):
    widths = band_widths.astype(jnp.float32)

    def one(index):
        volume = assemble(image[index].astype(jnp.float32))
        moment = assemble(momentum[index].astype(jnp.float32))
        flag = assemble(jnp.broadcast_to(tissue_flags[index].astype(jnp.float32)[:, None, None, None], (N_SPACE, CX, CY, CZ)))
        velocity = smooth_axis(moment, widths[0], 1)
        velocity = smooth_axis(velocity, widths[1], 2)
        velocity = smooth_axis(velocity, widths[2], 3)
        warped = volume
        for step in range(STEPS):
            flux = jnp.zeros_like(warped)
            for axis in range(3):
                lower, upper = neighbours(warped, axis)
                speed = velocity[axis]
                flux = flux + jnp.maximum(speed, 0.0) * (warped - lower) + jnp.minimum(speed, 0.0) * (upper - warped)
            warped = warped - (1.0 / STEPS) * flux
        divergence = jnp.zeros_like(warped)
        for axis in range(3):
            lower, upper = neighbours(velocity[axis], axis)
            divergence = divergence + 0.5 * (upper - lower)
        return warped, flag * jnp.exp(divergence)

    warped, weight = lax.map(one, jnp.arange(SUBJECTS))
    numer = jnp.sum(weight * warped, axis=0)
    denom = 1.0 + jnp.sum(weight, axis=0)
    template = numer / denom
    mismatch = (warped - template[None]).astype(jnp.bfloat16)
    return split_tiles(mismatch), split_tiles(template)
```

```python
import functools

import jax
import jax.numpy as jnp
from jax import lax
from jax.experimental import pallas as pl
from jax.experimental.pallas import tpu as pltpu
from jax.sharding import PartitionSpec as P

TGY = 4
STEPS = 4
CX = 24
CY = 48
CZ = 128
EDGE = 16
PAD = 8
MESH = pl.DeviceIdType.MESH
OWN = slice(PAD, PAD + CY)
N, S, W, E = range(4)


def kernel(
    wide,
    widths_ref,
    flags_ref,
    image_ref,
    moment_ref,
    mismatch_ref,
    template_ref,
    edge_out,
    edge_in,
    field,
    speed,
    warped,
    rows_in,
    cols_out,
    cols_in,
    vrows_in,
    vcols_out,
    vcols_in,
    weight,
    sums,
    pair_in,
    half,
    parts_in,
    whole,
    z_send,
    z_recv,
    y_send,
    y_recv,
    step_send,
    step_recv,
    v_send,
    v_recv,
    pair_send,
    pair_recv,
    part_send,
    part_recv,
    gather_send,
    gather_recv,
):
    subj = lax.axis_index("subj")
    space = lax.axis_index("space")
    row, col = space // TGY, space % TGY
    chip, core = subj // 2, subj % 2
    place = (
        (subj, ((row + 3) % 4) * TGY + col),
        (subj, ((row + 1) % 4) * TGY + col),
        (subj, row * TGY + (col + 3) % 4),
        (subj, row * TGY + (col + 1) % 4),
    )
    sibling = (chip * 2 + 1 - core, space)
    chips = [(chip + k) % 8 for k in range(1, 8)]
    peers = [(other * 2 + core, space) for other in chips]

    barrier = pltpu.get_barrier_semaphore()
    for device in list(place) + [sibling] + peers:
        pl.semaphore_signal(barrier, inc=1, device_id=device, device_id_type=MESH)

    has = tuple(
        jnp.where(flag, 1.0, 0.0).astype(jnp.float32)
        for flag in (row > 0, row < 3, col > 0, col < TGY - 1)
    )
    lane = lax.broadcasted_iota(jnp.int32, (8, CZ), 1)
    tiles = [(PAD + 8 * t, 8 * t) for t in range(CY // 8)]

    def remote(src, dst, send, recv, device):
        return pltpu.make_async_remote_copy(
            src_ref=src,
            dst_ref=dst,
            send_sem=send,
            recv_sem=recv,
            device_id=device,
            device_id_type=MESH,
        )

    def loop(body, count, unroll=1):
        def step(i, carry):
            body(i)
            return carry

        lax.fori_loop(0, count, step, 0, unroll=unroll)

    def stage_edges(c):
        def body(x):
            edge_out[c, 0, x] = moment_ref[c, x, 0:EDGE, :].astype(jnp.float32)
            edge_out[c, 1, x] = moment_ref[c, x, CY - EDGE : CY, :].astype(jnp.float32)

        loop(body, CX, 4)

    def stage_image(s):
        def body(x):
            value = image_ref[s, x].astype(jnp.float32)
            warped[s, 0, x + 1, OWN, :] = value
            cols_out[s, 0, 0, pl.ds(x, 1), :] = value[0:1]
            cols_out[s, 0, 1, pl.ds(x, 1), :] = value[CY - 1 : CY]

        loop(body, CX, 4)

    for c in range(6):
        stage_edges(c)
    for s in range(2):
        stage_image(s)
    pl.semaphore_wait(barrier, 12)

    def start_edges(c):
        pair = (
            remote(edge_out.at[c, 0], edge_in.at[c, 1], y_send.at[c, 0], y_recv.at[c, 0], place[W]),
            remote(edge_out.at[c, 1], edge_in.at[c, 0], y_send.at[c, 1], y_recv.at[c, 1], place[E]),
        )
        for copy in pair:
            copy.start()
        return pair

    def start_halo(s, k):
        slot = k % 2
        copies = (
            remote(warped.at[s, slot, 1, OWN], rows_in.at[s, k, 1], step_send.at[s, k, N], step_recv.at[s, k, N], place[N]),
            remote(warped.at[s, slot, CX, OWN], rows_in.at[s, k, 0], step_send.at[s, k, S], step_recv.at[s, k, S], place[S]),
            remote(cols_out.at[s, k, 0], cols_in.at[s, k, 1], step_send.at[s, k, W], step_recv.at[s, k, W], place[W]),
            remote(cols_out.at[s, k, 1], cols_in.at[s, k, 0], step_send.at[s, k, E], step_recv.at[s, k, E], place[E]),
        )
        for copy in copies:
            copy.start()
        return copies

    def start_speed(s):
        a, b = 3 * s, 3 * s + 1
        del b
        copies = (
            remote(speed.at[a, 1, OWN], vrows_in.at[s, 1], v_send.at[s, N], v_recv.at[s, N], place[N]),
            remote(speed.at[a, CX, OWN], vrows_in.at[s, 0], v_send.at[s, S], v_recv.at[s, S], place[S]),
            remote(vcols_out.at[s, 0], vcols_in.at[s, 1], v_send.at[s, W], v_recv.at[s, W], place[W]),
            remote(vcols_out.at[s, 1], vcols_in.at[s, 0], v_send.at[s, E], v_recv.at[s, E], place[E]),
        )
        for copy in copies:
            copy.start()
        return copies

    def start_bulk(c):
        copies = (
            remote(field.at[c, pl.ds(wide, wide)], field.at[c, pl.ds(wide + CX, wide)], z_send.at[c, 0], z_recv.at[c, 0], place[N]),
            remote(field.at[c, pl.ds(CX, wide)], field.at[c, pl.ds(0, wide)], z_send.at[c, 1], z_recv.at[c, 1], place[S]),
        )
        for copy in copies:
            copy.start()
        return copies

    edges = [start_edges(0)]
    halos = {(s, 0): start_halo(s, 0) for s in range(2)}
    edges += [start_edges(c) for c in range(1, 6)]

    width = [widths_ref[a].astype(jnp.float32) for a in range(3)]
    out_id = lax.broadcasted_iota(jnp.int32, (CY, CY + 2 * EDGE), 0)
    in_id = lax.broadcasted_iota(jnp.int32, (CY, CY + 2 * EDGE), 1)
    dist = jnp.abs(in_id - EDGE - out_id).astype(jnp.float32)
    second = jnp.maximum(width[1] + 1.0 - dist, 0.0)
    second = jnp.where(in_id < EDGE, second * has[W], second)
    second = jnp.where(in_id >= EDGE + CY, second * has[E], second)
    second = second.astype(jnp.bfloat16)
    out_id = lax.broadcasted_iota(jnp.int32, (CZ, CZ), 0)
    in_id = lax.broadcasted_iota(jnp.int32, (CZ, CZ), 1)
    dist = jnp.abs(in_id - out_id).astype(jnp.float32)
    third = jnp.maximum(width[2] + 1.0 - dist, 0.0).astype(jnp.bfloat16)
    norm = 1.0
    for a in range(3):
        norm = norm * ((width[a] + 1.0) * (width[a] + 1.0))
    scale = jnp.full((8, CZ), 1.0 / STEPS, jnp.float32) / jnp.full((8, CZ), 1.0, jnp.float32) / norm

    def smooth_inner(c):
        group = 4

        def body(g):
            blocks = []
            for j in range(group):
                x = g * group + j
                ext = jnp.concatenate(
                    [
                        edge_in[c, 0, x].astype(jnp.bfloat16),
                        moment_ref[c, x],
                        edge_in[c, 1, x].astype(jnp.bfloat16),
                    ],
                    axis=0,
                )
                blocks.append(jnp.dot(second, ext, preferred_element_type=jnp.float32))
            value = jnp.concatenate(blocks, axis=0)
            high = value.astype(jnp.bfloat16)
            low = (value - high.astype(jnp.float32)).astype(jnp.bfloat16)
            value = jnp.dot(high, third, preferred_element_type=jnp.float32) + jnp.dot(
                low, third, preferred_element_type=jnp.float32
            )
            for j in range(group):
                field[c, wide + g * group + j] = value[j * CY : (j + 1) * CY]

        loop(body, CX // group)

    def smooth_first(c):
        s, a = c // 3, c % 3

        def at(i, t, side=None):
            value = field[c, i, t : t + 8, :]
            return value if side is None else value * has[side]

        total, slope = [], []
        for _, t in tiles:
            sides = [N] * wide + [None] * CX
            first = [at(i, t, sides[i]) for i in range(2 * wide + 2)]
            total.append(sum((wide + 1.0 - abs(i - wide)) * first[i] for i in range(2 * wide + 1)))
            slope.append(sum(first[wide + 1 : 2 * wide + 2]) - sum(first[0 : wide + 1]))

        def emit(x, values):
            for (p, _), value in zip(tiles, values):
                speed[c, x + 1, p : p + 8, :] = value * scale
            if a == 1:
                vcols_out[s, 0, pl.ds(x, 1), :] = (values[0] * scale)[0:1]
                vcols_out[s, 1, pl.ds(x, 1), :] = (values[-1] * scale)[7:8]

        def advance(low, high):
            def step(i, carry):
                total, slope = carry
                emit(i, total)
                total = [p + q for p, q in zip(total, slope)]
                ahead = jnp.where(i + 2 * wide + 2 >= wide + CX, has[S], 1.0)
                behind = jnp.where(i < wide, has[N], 1.0)
                slope = [
                    q + (at(i + 2 * wide + 2, t) * ahead + at(i, t) * behind - 2.0 * at(i + wide + 1, t))
                    for q, (_, t) in zip(slope, tiles)
                ]
                return total, slope

            return lambda carry: lax.fori_loop(low, high, step, carry)

        total, slope = advance(0, CX - 2)((total, slope))
        emit(CX - 2, total)
        emit(CX - 1, [p + q for p, q in zip(total, slope)])

    def side_columns(target, columns, x):
        target[x + 1, PAD - 1 : PAD, :] = columns[0, pl.ds(x, 1), :] * has[W]
        target[x + 1, PAD + CY : PAD + CY + 1, :] = columns[1, pl.ds(x, 1), :] * has[E]

    def side_rows(target, rows):
        target[0, OWN, :] = rows[0] * has[N]
        target[CX + 1, OWN, :] = rows[1] * has[S]

    def transport(s, k, after):
        held, made = warped.at[s, k % 2], warped.at[s, (k + 1) % 2]
        side_rows(held, rows_in.at[s, k])

        def body(x):
            side_columns(held, cols_in.at[s, k], x)
            values = []
            for p, _ in tiles:
                centre = held[x + 1, p : p + 8, :]
                below = jnp.where(lane == 0, 0.0, pltpu.roll(centre, 1, 1))
                above = jnp.where(lane == CZ - 1, 0.0, pltpu.roll(centre, CZ - 1, 1))
                sides = (
                    (held[x, p : p + 8, :], held[x + 2, p : p + 8, :]),
                    (held[x + 1, p - 1 : p + 7, :], held[x + 1, p + 1 : p + 9, :]),
                    (below, above),
                )
                value = centre
                for a in range(3):
                    rate = speed[3 * s + a, x + 1, p : p + 8, :]
                    lower, upper = sides[a]
                    value = value - jnp.abs(rate) * (centre - jnp.where(rate > 0.0, lower, upper))
                made[x + 1, p : p + 8, :] = value
                values.append(value)
            after(x, values)

        loop(body, CX, 2)

    def stage_columns(s, k):
        def after(x, values):
            cols_out[s, k, 0, pl.ds(x, 1), :] = values[0][0:1]
            cols_out[s, k, 1, pl.ds(x, 1), :] = values[-1][7:8]

        return after

    def wait(copies):
        for copy in copies:
            copy.wait()

    def weigh(s):
        first, middle, last = (speed.at[3 * s + a] for a in range(3))
        side_rows(first, vrows_in.at[s])
        flag = flags_ref[s].astype(jnp.float32)

        def body(x):
            side_columns(middle, vcols_in.at[s], x)
            for p, t in tiles:
                centre = last[x + 1, p : p + 8, :]
                below = jnp.where(lane == 0, 0.0, pltpu.roll(centre, 1, 1))
                above = jnp.where(lane == CZ - 1, 0.0, pltpu.roll(centre, CZ - 1, 1))
                total = first[x + 2, p : p + 8, :] - first[x, p : p + 8, :]
                total = total + (middle[x + 1, p + 1 : p + 9, :] - middle[x + 1, p - 1 : p + 7, :])
                total = total + (above - below)
                value = flag * jnp.exp(total * (0.5 * STEPS))
                weight[s, x, t : t + 8, :] = value
                if s == 0:
                    sums[1, x, t : t + 8, :] = value
                else:
                    sums[1, x, t : t + 8, :] += value

        loop(body, CX, 2)

    mine = pl.multiple_of(24 * core, 8)
    theirs = pl.multiple_of(24 * (1 - core), 8)

    def start_pair(q):
        copy = remote(sums.at[q, :, pl.ds(theirs, 24)], pair_in.at[q], pair_send.at[q], pair_recv.at[q], sibling)
        copy.start()
        return copy

    def start_parts(q):
        def body(x):
            half[q, x] = sums[q, x, pl.ds(mine, 24), :] + pair_in[q, x]

        loop(body, CX, 4)
        copies = [
            remote(half.at[q, pl.ds(3 * other, 3)], parts_in.at[q, k], part_send.at[q, k], part_recv.at[q, k], peers[k])
            for k, other in enumerate(chips)
        ]
        for copy in copies:
            copy.start()
        return copies

    bulk = {}
    for c in range(6):
        wait(edges[c])
        smooth_inner(c)
        if c < 4:
            bulk[c] = start_bulk(c)
    for c in range(3):
        wait(bulk[c])
        smooth_first(c)
    for k in range(4):
        wait(halos[0, k])
        if k == 1:
            wait(shift)
        if k < 3:
            transport(0, k, stage_columns(0, k + 1))
            halos[0, k + 1] = start_halo(0, k + 1)
            if k == 0:
                shift = start_speed(0)
            if k < 2:
                bulk[4 + k] = start_bulk(4 + k)
        else:
            transport(0, k, lambda x, values: None)
        if k == 1:
            weigh(0)
            wait(bulk[3])
            smooth_first(3)
        if k == 2:
            wait(bulk[4])
            smooth_first(4)

    wait(bulk[5])
    smooth_first(5)
    wait(halos[1, 0])
    transport(1, 0, stage_columns(1, 1))
    halos[1, 1] = start_halo(1, 1)
    shift = start_speed(1)
    wait(halos[1, 1])
    transport(1, 1, stage_columns(1, 2))
    halos[1, 2] = start_halo(1, 2)
    wait(shift)
    weigh(1)
    pair = start_pair(1)
    wait(halos[1, 2])
    transport(1, 2, stage_columns(1, 3))
    halos[1, 3] = start_halo(1, 3)
    pair.wait()
    parts = start_parts(1)
    wait(halos[1, 3])

    def gather_sum(x, values):
        for (p, t), value in zip(tiles, values):
            sums[0, x, t : t + 8, :] = (
                weight[0, x, t : t + 8, :] * warped[0, 0, x + 1, p : p + 8, :] + weight[1, x, t : t + 8, :] * value
            )

    transport(1, 3, gather_sum)
    pair = start_pair(0)
    wait(parts)
    pair.wait()
    wait(start_parts(0))

    own = 3 * chip
    for x in range(3):
        total = [half[q, own + x] for q in range(2)]
        for q in range(2):
            for k in range(7):
                total[q] = total[q] + parts_in[q, k, x]
        whole[own + x, pl.ds(mine, 24), :] = total[0] / (1.0 + total[1])

    def piece(other):
        return whole.at[pl.ds(3 * other, 3), pl.ds(mine, 24)]

    copies = [remote(piece(chip), piece(chip), gather_send.at[k], gather_recv.at[k], peers[k]) for k in range(7)]
    onward = [remote(piece(chip), piece(chip), gather_send.at[7], gather_recv.at[7], sibling)]
    for copy in copies + onward:
        copy.start()
    for k in range(7):
        copies[k].wait_recv()
        block = piece((chip + 7 - k) % 8)
        onward.append(remote(block, block, gather_send.at[8 + k], gather_recv.at[8 + k], sibling))
        onward[-1].start()
    for copy in copies:
        copy.wait_send()
    wait(onward)

    def finish(x):
        value = whole[x]
        template_ref[x] = value
        for s in range(2):
            mismatch_ref[s, x] = (warped[s, 0, x + 1, OWN, :] - value).astype(jnp.bfloat16)

    loop(finish, CX, 4)


def build(index, wide):
    f32 = jnp.float32
    dma = pltpu.SemaphoreType.DMA
    return pl.pallas_call(
        functools.partial(kernel, wide),
        out_shape=(
            jax.ShapeDtypeStruct((2, CX, CY, CZ), jnp.bfloat16),
            jax.ShapeDtypeStruct((CX, CY, CZ), f32),
        ),
        in_specs=[pl.BlockSpec(memory_space=pltpu.SMEM)] * 2 + [pl.BlockSpec(memory_space=pltpu.VMEM)] * 2,
        out_specs=(pl.BlockSpec(memory_space=pltpu.VMEM),) * 2,
        scratch_shapes=[
            pltpu.VMEM((6, 2, CX, EDGE, CZ), f32),
            pltpu.VMEM((6, 2, CX, EDGE, CZ), f32),
            pltpu.VMEM((6, CX + 2 * wide, CY, CZ), f32),
            pltpu.VMEM((6, CX + 2, CY + 2 * PAD, CZ), f32),
            pltpu.VMEM((2, 2, CX + 2, CY + 2 * PAD, CZ), f32),
            pltpu.VMEM((2, 4, 2, CY, CZ), f32),
            pltpu.VMEM((2, 4, 2, CX, CZ), f32),
            pltpu.VMEM((2, 4, 2, CX, CZ), f32),
            pltpu.VMEM((2, 2, CY, CZ), f32),
            pltpu.VMEM((2, 2, CX, CZ), f32),
            pltpu.VMEM((2, 2, CX, CZ), f32),
            pltpu.VMEM((2, CX, CY, CZ), f32),
            pltpu.VMEM((2, CX, CY, CZ), f32),
            pltpu.VMEM((2, CX, 24, CZ), f32),
            pltpu.VMEM((2, CX, 24, CZ), f32),
            pltpu.VMEM((2, 7, 3, 24, CZ), f32),
            pltpu.VMEM((CX, CY, CZ), f32),
            dma((6, 2)),
            dma((6, 2)),
            dma((6, 2)),
            dma((6, 2)),
            dma((2, 4, 4)),
            dma((2, 4, 4)),
            dma((2, 4)),
            dma((2, 4)),
            dma((2,)),
            dma((2,)),
            dma((2, 7)),
            dma((2, 7)),
            dma((15,)),
            dma((15,)),
        ],
        compiler_params=pltpu.CompilerParams(
            collective_id=index, has_side_effects=True, vmem_limit_bytes=48 * 2**20
        ),
    )


def per_device(image, momentum, tissue_flags, band_widths):
    args = (
        band_widths,
        tissue_flags.reshape(2),
        image.reshape(2, CX, CY, CZ),
        momentum.reshape(6, CX, CY, CZ),
    )
    which = jnp.clip((band_widths[0] - 8) // 2, 0, 2)
    mismatch, template = lax.switch(which, [build(i, 8 + 2 * i) for i in range(3)], *args)
    return mismatch[:, None], template[None]


def solution(mesh):
    return jax.shard_map(
        per_device,
        mesh=mesh,
        in_specs=(
            P("subj", "space", None, None, None),
            P("subj", None, "space", None, None, None),
            P("subj", "space"),
            P(),
        ),
        out_specs=(P("subj", "space", None, None, None), P("space", None, None, None)),
        check_vma=False,
    )
```

```python
import functools

import jax
import jax.numpy as jnp
from jax import lax
from jax.experimental import pallas as pl
from jax.experimental.pallas import tpu as pltpu
from jax.sharding import PartitionSpec as P

TGY = 4
STEPS = 4
CX = 24
CY = 48
CZ = 128
EDGE = 16
PAD = 8
MESH = pl.DeviceIdType.MESH
OWN = slice(PAD, PAD + CY)
N, S, W, E = range(4)


def kernel(
    wide,
    widths_ref,
    flags_ref,
    image_hbm,
    moment_hbm,
    mismatch_ref,
    template_ref,
    image_ref,
    moment_ref,
    edge_out,
    edge_in,
    field,
    middle_field,
    speed,
    warped,
    rows_in,
    cols_out,
    cols_in,
    vrows_in,
    vcols_out,
    vcols_in,
    weight,
    sums,
    pair_in,
    half,
    parts_in,
    denom_in,
    whole,
    load,
    z_send,
    z_recv,
    y_send,
    y_recv,
    step_send,
    step_recv,
    v_send,
    v_recv,
    pair_send,
    pair_recv,
    part_send,
    part_recv,
    denom_send,
    denom_recv,
    gather_send,
    gather_recv,
):
    subj = lax.axis_index("subj")
    space = lax.axis_index("space")
    row, col = space // TGY, space % TGY
    chip, core = subj // 2, subj % 2
    place = (
        (subj, ((row + 3) % 4) * TGY + col),
        (subj, ((row + 1) % 4) * TGY + col),
        (subj, row * TGY + (col + 3) % 4),
        (subj, row * TGY + (col + 1) % 4),
    )
    owners = [((chip + b // 2 + 1) % 8, core if b % 2 == 0 else 1 - core) for b in range(14)]
    owners.append((chip, 1 - core))
    peers = [(chip_at * 2 + core_at, space) for chip_at, core_at in owners]

    barrier = pltpu.get_barrier_semaphore()
    for device in list(place) + peers:
        pl.semaphore_signal(barrier, inc=1, device_id=device, device_id_type=MESH)
    loads = [pltpu.make_async_copy(moment_hbm.at[c], moment_ref.at[c], load.at[c]) for c in range(6)]
    loads.append(pltpu.make_async_copy(image_hbm, image_ref, load.at[6]))
    for copy in loads:
        copy.start()

    has = tuple(
        jnp.where(flag, 1.0, 0.0).astype(jnp.float32)
        for flag in (row > 0, row < 3, col > 0, col < TGY - 1)
    )
    lane = lax.broadcasted_iota(jnp.int32, (8, CZ), 1)
    tiles = [(PAD + 8 * t, 8 * t) for t in range(CY // 8)]

    def remote(src, dst, send, recv, device):
        return pltpu.make_async_remote_copy(
            src_ref=src,
            dst_ref=dst,
            send_sem=send,
            recv_sem=recv,
            device_id=device,
            device_id_type=MESH,
        )

    def loop(body, count, unroll=1):
        def step(i, carry):
            body(i)
            return carry

        lax.fori_loop(0, count, step, 0, unroll=unroll)

    def stage_edges(c):
        def body(x):
            edge_out[c, 0, x] = moment_ref[c, x, 0:EDGE, :].astype(jnp.float32)
            edge_out[c, 1, x] = moment_ref[c, x, CY - EDGE : CY, :].astype(jnp.float32)

        loop(body, CX, 8)

    def stage_image(s):
        def body(x):
            value = image_ref[s, x].astype(jnp.float32)
            warped[s, 0, x + 1, OWN, :] = value
            cols_out[s, 0, 0, pl.ds(x, 1), :] = value[0:1]
            cols_out[s, 0, 1, pl.ds(x, 1), :] = value[CY - 1 : CY]

        loop(body, CX, 4)

    def stage_first(x):
        field[0, wide + x] = moment_ref[0, x].astype(jnp.float32)

    loads[0].wait()
    loop(stage_first, CX, 8)
    for c in range(1, 4):
        loads[c].wait()
        stage_edges(c)
    pl.semaphore_wait(barrier, 19)

    def start_edges(c):
        pair = (
            remote(edge_out.at[c, 0], edge_in.at[c, 1], y_send.at[c, 0], y_recv.at[c, 0], place[W]),
            remote(edge_out.at[c, 1], edge_in.at[c, 0], y_send.at[c, 1], y_recv.at[c, 1], place[E]),
        )
        for copy in pair:
            copy.start()
        return pair

    def start_halo(s, k):
        slot = k % 2
        copies = (
            remote(warped.at[s, slot, 1, OWN], rows_in.at[s, k, 1], step_send.at[s, k, N], step_recv.at[s, k, N], place[N]),
            remote(warped.at[s, slot, CX, OWN], rows_in.at[s, k, 0], step_send.at[s, k, S], step_recv.at[s, k, S], place[S]),
            remote(cols_out.at[s, k, 0], cols_in.at[s, k, 1], step_send.at[s, k, W], step_recv.at[s, k, W], place[W]),
            remote(cols_out.at[s, k, 1], cols_in.at[s, k, 0], step_send.at[s, k, E], step_recv.at[s, k, E], place[E]),
        )
        for copy in copies:
            copy.start()
        return copies

    def start_speed_rows(s):
        a = 3 * s
        copies = (
            remote(speed.at[a, 1, OWN], vrows_in.at[s, 1], v_send.at[s, N], v_recv.at[s, N], place[N]),
            remote(speed.at[a, CX, OWN], vrows_in.at[s, 0], v_send.at[s, S], v_recv.at[s, S], place[S]),
        )
        for copy in copies:
            copy.start()
        return copies

    def start_speed_cols(s):
        copies = (
            remote(vcols_out.at[s, 0], vcols_in.at[s, 1], v_send.at[s, W], v_recv.at[s, W], place[W]),
            remote(vcols_out.at[s, 1], vcols_in.at[s, 0], v_send.at[s, E], v_recv.at[s, E], place[E]),
        )
        for copy in copies:
            copy.start()
        return copies

    def start_bulk(c):
        copies = (
            remote(field.at[c, pl.ds(wide, wide)], field.at[c, pl.ds(wide + CX, wide)], z_send.at[c, 0], z_recv.at[c, 0], place[N]),
            remote(field.at[c, pl.ds(CX, wide)], field.at[c, pl.ds(0, wide)], z_send.at[c, 1], z_recv.at[c, 1], place[S]),
        )
        for copy in copies:
            copy.start()
        return copies

    def start_middle():
        copies = (
            remote(middle_field.at[:, 0:EDGE], edge_in.at[0, 1], y_send.at[0, 0], y_recv.at[0, 0], place[W]),
            remote(middle_field.at[:, CY - EDGE : CY], edge_in.at[0, 0], y_send.at[0, 1], y_recv.at[0, 1], place[E]),
        )
        for copy in copies:
            copy.start()
        return copies

    edges = {1: start_edges(1)}
    bulk = {0: start_bulk(0)}
    for c in range(2, 4):
        edges[c] = start_edges(c)
    for c in range(4, 6):
        loads[c].wait()
        stage_edges(c)
    loads[6].wait()
    for s in range(2):
        stage_image(s)

    width = [widths_ref[a].astype(jnp.float32) for a in range(3)]
    out_id = lax.broadcasted_iota(jnp.int32, (CY, CY + 2 * EDGE), 0)
    in_id = lax.broadcasted_iota(jnp.int32, (CY, CY + 2 * EDGE), 1)
    dist = jnp.abs(in_id - EDGE - out_id).astype(jnp.float32)
    second = jnp.maximum(width[1] + 1.0 - dist, 0.0)
    second = jnp.where(in_id < EDGE, second * has[W], second)
    second = jnp.where(in_id >= EDGE + CY, second * has[E], second)
    second = second.astype(jnp.bfloat16)
    out_id = lax.broadcasted_iota(jnp.int32, (CZ, CZ), 0)
    in_id = lax.broadcasted_iota(jnp.int32, (CZ, CZ), 1)
    dist = jnp.abs(in_id - out_id).astype(jnp.float32)
    third = jnp.maximum(width[2] + 1.0 - dist, 0.0).astype(jnp.bfloat16)
    norm = 1.0
    for a in range(3):
        norm = norm * ((width[a] + 1.0) * (width[a] + 1.0))
    scale = jnp.full((8, CZ), 1.0 / STEPS, jnp.float32) / jnp.full((8, CZ), 1.0, jnp.float32) / norm

    def smooth_inner(c):
        group = 12

        def body(g):
            blocks = []
            for j in range(group):
                x = g * group + j
                ext = jnp.concatenate(
                    [
                        edge_in[c, 0, x].astype(jnp.bfloat16),
                        moment_ref[c, x],
                        edge_in[c, 1, x].astype(jnp.bfloat16),
                    ],
                    axis=0,
                )
                blocks.append(jnp.dot(second, ext, preferred_element_type=jnp.float32))
            value = jnp.concatenate(blocks, axis=0)
            high = value.astype(jnp.bfloat16)
            low = (value - high.astype(jnp.float32)).astype(jnp.bfloat16)
            value = jnp.dot(high, third, preferred_element_type=jnp.float32) + jnp.dot(
                low, third, preferred_element_type=jnp.float32
            )
            for j in range(group):
                field[c, wide + g * group + j] = value[j * CY : (j + 1) * CY]

        loop(body, CX // group)

    def split(value):
        high = value.astype(jnp.bfloat16)
        return high, (value - high.astype(jnp.float32)).astype(jnp.bfloat16)

    def smooth_inner_last():
        group = 12

        def body(g):
            blocks = []
            for j in range(group):
                x = g * group + j
                ext = jnp.concatenate([edge_in[0, 0, x], middle_field[x], edge_in[0, 1, x]], axis=0)
                blocks.append(
                    sum(jnp.dot(second, part, preferred_element_type=jnp.float32) for part in split(ext))
                )
            value = jnp.concatenate(blocks, axis=0)
            value = sum(jnp.dot(part, third, preferred_element_type=jnp.float32) for part in split(value))
            for j in range(group):
                speed[0, g * group + j + 1, OWN, :] = value[j * CY : (j + 1) * CY] * scale[0:1]

        loop(body, CX // group)

    def smooth_first(c):
        s, a = c // 3, c % 3

        def at(i, t, side=None):
            value = field[c, i, t : t + 8, :]
            return value if side is None else value * has[side]

        total, slope = [], []
        for _, t in tiles:
            sides = [N] * wide + [None] * CX
            first = [at(i, t, sides[i]) for i in range(2 * wide + 2)]
            total.append(sum((wide + 1.0 - abs(i - wide)) * first[i] for i in range(2 * wide + 1)))
            slope.append(sum(first[wide + 1 : 2 * wide + 2]) - sum(first[0 : wide + 1]))

        def emit(x, values):
            for (p, t), value in zip(tiles, values):
                if c == 0:
                    middle_field[x, t : t + 8, :] = value
                else:
                    speed[c, x + 1, p : p + 8, :] = value * scale
            if a == 1:
                vcols_out[s, 0, pl.ds(x, 1), :] = (values[0] * scale)[0:1]
                vcols_out[s, 1, pl.ds(x, 1), :] = (values[-1] * scale)[7:8]

        def advance(low, high):
            def step(i, carry):
                total, slope = carry
                emit(i, total)
                total = [p + q for p, q in zip(total, slope)]
                ahead = jnp.where(i + 2 * wide + 2 >= wide + CX, has[S], 1.0)
                behind = jnp.where(i < wide, has[N], 1.0)
                slope = [
                    q + (at(i + 2 * wide + 2, t) * ahead + at(i, t) * behind - 2.0 * at(i + wide + 1, t))
                    for q, (_, t) in zip(slope, tiles)
                ]
                return total, slope

            return lambda carry: lax.fori_loop(low, high, step, carry, unroll=2)

        total, slope = advance(0, CX - 2)((total, slope))
        emit(CX - 2, total)
        emit(CX - 1, [p + q for p, q in zip(total, slope)])

    def side_columns(target, columns, x):
        target[x + 1, PAD - 1 : PAD, :] = columns[0, pl.ds(x, 1), :] * has[W]
        target[x + 1, PAD + CY : PAD + CY + 1, :] = columns[1, pl.ds(x, 1), :] * has[E]

    def side_rows(target, rows):
        target[0, OWN, :] = rows[0] * has[N]
        target[CX + 1, OWN, :] = rows[1] * has[S]

    def transport(s, k, after, blocks=None):
        held, made = warped.at[s, k % 2], warped.at[s, (k + 1) % 2]
        side_rows(held, rows_in.at[s, k])

        def body(x):
            side_columns(held, cols_in.at[s, k], x)
            values = []
            for p, _ in tiles:
                centre = held[x + 1, p : p + 8, :]
                below = jnp.where(lane == 0, 0.0, pltpu.roll(centre, 1, 1))
                above = jnp.where(lane == CZ - 1, 0.0, pltpu.roll(centre, CZ - 1, 1))
                sides = (
                    (held[x, p : p + 8, :], held[x + 2, p : p + 8, :]),
                    (held[x + 1, p - 1 : p + 7, :], held[x + 1, p + 1 : p + 9, :]),
                    (below, above),
                )
                value = centre
                for a in range(3):
                    rate = speed[3 * s + a, x + 1, p : p + 8, :]
                    lower, upper = sides[a]
                    value = value - jnp.abs(rate) * (centre - jnp.where(rate > 0.0, lower, upper))
                made[x + 1, p : p + 8, :] = value
                values.append(value)
            after(x, values)

        if blocks is None:
            loop(body, CX, 8)
        else:
            for b, block in enumerate(blocks):
                loop(lambda r: body(3 * block + r), 3, 3)
                send_numer(b)

    def stage_columns(s, k):
        def after(x, values):
            cols_out[s, k, 0, pl.ds(x, 1), :] = values[0][0:1]
            cols_out[s, k, 1, pl.ds(x, 1), :] = values[-1][7:8]

        return after

    def wait(copies):
        for copy in copies:
            copy.wait()

    def weigh(s):
        first, middle, last = (speed.at[3 * s + a] for a in range(3))
        side_rows(first, vrows_in.at[s])
        flag = flags_ref[s].astype(jnp.float32)

        def body(x):
            side_columns(middle, vcols_in.at[s], x)
            for p, t in tiles:
                centre = last[x + 1, p : p + 8, :]
                below = jnp.where(lane == 0, 0.0, pltpu.roll(centre, 1, 1))
                above = jnp.where(lane == CZ - 1, 0.0, pltpu.roll(centre, CZ - 1, 1))
                total = first[x + 2, p : p + 8, :] - first[x, p : p + 8, :]
                total = total + (middle[x + 1, p + 1 : p + 9, :] - middle[x + 1, p - 1 : p + 7, :])
                total = total + (above - below)
                value = flag * jnp.exp(total * (0.5 * STEPS))
                weight[s, x, t : t + 8, :] = value
                if s == 0:
                    sums[1, x, t : t + 8, :] = value
                else:
                    sums[1, x, t : t + 8, :] += value

        loop(body, CX, 8)

    def piece(ref, chip_at, core_at):
        return ref.at[pl.ds(3 * chip_at, 3), pl.ds(pl.multiple_of(24 * core_at, 8), 24)]

    def send_numer(b):
        for k in (2 * b, 2 * b + 1):
            if k == 15:
                continue
            block = piece(sums.at[0], *owners[k])
            copy = remote(block, parts_in.at[k], part_send.at[k], part_recv.at[k], peers[k])
            copy.start()
            numer_parts.append(copy)

    numer_parts = []
    here = pl.multiple_of(24 * core, 8)
    there = pl.multiple_of(24 * (1 - core), 8)

    def start_pair():
        copy = remote(sums.at[1, :, pl.ds(there, 24)], pair_in, pair_send.at[0], pair_recv.at[0], peers[14])
        copy.start()
        return copy

    def add_pair():
        def body(x):
            half[x] = sums[1, x, pl.ds(here, 24), :] + pair_in[x]

        loop(body, CX, 8)

    def start_denom():
        copies = [
            remote(half.at[pl.ds(3 * owners[2 * b][0], 3)], denom_in.at[b], denom_send.at[b], denom_recv.at[b], peers[2 * b])
            for b in range(7)
        ]
        for copy in copies:
            copy.start()
        return copies

    wait(edges[1])
    smooth_inner(1)
    bulk[1] = start_bulk(1)
    halos = {(s, 0): start_halo(s, 0) for s in range(2)}
    wait(edges[2])
    smooth_inner(2)
    bulk[2] = start_bulk(2)
    wait(bulk[0])
    smooth_first(0)
    edges[0] = start_middle()
    edges[4] = start_edges(4)
    edges[5] = start_edges(5)
    wait(edges[3])
    smooth_inner(3)
    bulk[3] = start_bulk(3)
    wait(bulk[1])
    smooth_first(1)
    shift = {0: start_speed_cols(0)}
    wait(edges[0])
    smooth_inner_last()
    shift[0] += start_speed_rows(0)
    wait(edges[4])
    smooth_inner(4)
    wait(edges[5])
    smooth_inner(5)
    wait(bulk[2])
    smooth_first(2)
    wait(halos[0, 0])
    transport(0, 0, stage_columns(0, 1))
    halos[0, 1] = start_halo(0, 1)
    bulk[4] = start_bulk(4)
    wait(bulk[3])
    smooth_first(3)
    shift[1] = start_speed_rows(1)
    wait(halos[0, 1])
    transport(0, 1, stage_columns(0, 2))
    halos[0, 2] = start_halo(0, 2)
    bulk[5] = start_bulk(5)
    wait(shift[0])
    weigh(0)
    wait(halos[0, 2])
    transport(0, 2, stage_columns(0, 3))
    halos[0, 3] = start_halo(0, 3)
    wait(bulk[4])
    smooth_first(4)
    shift[1] += start_speed_cols(1)
    wait(halos[1, 0])

    wait(bulk[5])
    smooth_first(5)
    transport(1, 0, stage_columns(1, 1))
    halos[1, 1] = start_halo(1, 1)
    wait(shift[1])
    weigh(1)
    pair = start_pair()
    wait(halos[0, 3])
    transport(0, 3, lambda x, values: None)
    wait(halos[1, 1])
    transport(1, 1, stage_columns(1, 2))
    halos[1, 2] = start_halo(1, 2)
    pair.wait()
    add_pair()
    wait(halos[1, 2])
    transport(1, 2, stage_columns(1, 3))
    halos[1, 3] = start_halo(1, 3)
    denom_parts = start_denom()
    wait(halos[1, 3])

    def gather_sum(x, values):
        for (p, t), value in zip(tiles, values):
            sums[0, x, t : t + 8, :] = (
                weight[0, x, t : t + 8, :] * warped[0, 0, x + 1, p : p + 8, :] + weight[1, x, t : t + 8, :] * value
            )

    transport(1, 3, gather_sum, [owners[2 * b][0] for b in range(7)] + [chip])
    wait(denom_parts)
    denom = []
    for x in range(3):
        total = half[3 * chip + x]
        for k in range(7):
            total = total + denom_in[k, x]
        denom.append(1.0 + total)
    wait(numer_parts)
    for x in range(3):
        total = sums[0, 3 * chip + x, pl.ds(here, 24), :]
        for k in range(15):
            total = total + parts_in[k, x]
        whole[3 * chip + x, pl.ds(here, 24), :] = total / denom[x]

    own = piece(whole, chip, core)
    copies = [remote(own, own, gather_send.at[k], gather_recv.at[k], peers[k]) for k in range(15)]
    for copy in copies:
        copy.start()
    wait(copies)

    def finish(x):
        value = whole[x]
        template_ref[x] = value
        for s in range(2):
            mismatch_ref[s, x] = (warped[s, 0, x + 1, OWN, :] - value).astype(jnp.bfloat16)

    loop(finish, CX, 8)


def build(index, wide):
    f32 = jnp.float32
    dma = pltpu.SemaphoreType.DMA
    return pl.pallas_call(
        functools.partial(kernel, wide),
        out_shape=(
            jax.ShapeDtypeStruct((2, CX, CY, CZ), jnp.bfloat16),
            jax.ShapeDtypeStruct((CX, CY, CZ), f32),
        ),
        in_specs=[pl.BlockSpec(memory_space=pltpu.SMEM)] * 2 + [pl.BlockSpec(memory_space=pl.ANY)] * 2,
        out_specs=(pl.BlockSpec(memory_space=pltpu.VMEM),) * 2,
        scratch_shapes=[
            pltpu.VMEM((2, CX, CY, CZ), jnp.bfloat16),
            pltpu.VMEM((6, CX, CY, CZ), jnp.bfloat16),
            pltpu.VMEM((6, 2, CX, EDGE, CZ), f32),
            pltpu.VMEM((6, 2, CX, EDGE, CZ), f32),
            pltpu.VMEM((6, CX + 2 * wide, CY, CZ), f32),
            pltpu.VMEM((CX, CY, CZ), f32),
            pltpu.VMEM((6, CX + 2, CY + 2 * PAD, CZ), f32),
            pltpu.VMEM((2, 2, CX + 2, CY + 2 * PAD, CZ), f32),
            pltpu.VMEM((2, 4, 2, CY, CZ), f32),
            pltpu.VMEM((2, 4, 2, CX, CZ), f32),
            pltpu.VMEM((2, 4, 2, CX, CZ), f32),
            pltpu.VMEM((2, 2, CY, CZ), f32),
            pltpu.VMEM((2, 2, CX, CZ), f32),
            pltpu.VMEM((2, 2, CX, CZ), f32),
            pltpu.VMEM((2, CX, CY, CZ), f32),
            pltpu.VMEM((2, CX, CY, CZ), f32),
            pltpu.VMEM((CX, 24, CZ), f32),
            pltpu.VMEM((CX, 24, CZ), f32),
            pltpu.VMEM((15, 3, 24, CZ), f32),
            pltpu.VMEM((7, 3, 24, CZ), f32),
            pltpu.VMEM((CX, CY, CZ), f32),
            dma((7,)),
            dma((6, 2)),
            dma((6, 2)),
            dma((6, 2)),
            dma((6, 2)),
            dma((2, 4, 4)),
            dma((2, 4, 4)),
            dma((2, 4)),
            dma((2, 4)),
            dma((1,)),
            dma((1,)),
            dma((15,)),
            dma((15,)),
            dma((7,)),
            dma((7,)),
            dma((15,)),
            dma((15,)),
        ],
        compiler_params=pltpu.CompilerParams(
            collective_id=index, has_side_effects=True, vmem_limit_bytes=48 * 2**20
        ),
    )


def per_device(image, momentum, tissue_flags, band_widths):
    args = (
        band_widths,
        tissue_flags.reshape(2),
        image.reshape(2, CX, CY, CZ),
        momentum.reshape(6, CX, CY, CZ),
    )
    which = jnp.clip((band_widths[0] - 8) // 2, 0, 2)
    mismatch, template = lax.switch(which, [build(i, 8 + 2 * i) for i in range(3)], *args)
    return mismatch[:, None], template[None]


def solution(mesh):
    return jax.shard_map(
        per_device,
        mesh=mesh,
        in_specs=(
            P("subj", "space", None, None, None),
            P("subj", None, "space", None, None, None),
            P("subj", "space"),
            P(),
        ),
        out_specs=(P("subj", "space", None, None, None), P("space", None, None, None)),
        check_vma=False,
    )
```

```python
import functools

import jax
import jax.numpy as jnp
from jax import lax
from jax.experimental import pallas as pl
from jax.experimental.pallas import tpu as pltpu
from jax.sharding import PartitionSpec as P

TGY = 4
STEPS = 4
CX = 24
CY = 48
CZ = 128
EDGE = 16
PAD = 8
MESH = pl.DeviceIdType.MESH
OWN = slice(PAD, PAD + CY)
N, S, W, E = range(4)


def kernel(
    wide,
    widths_ref,
    flags_ref,
    image_hbm,
    moment_hbm,
    mismatch_ref,
    template_ref,
    image_ref,
    moment_ref,
    edge_out,
    edge_in,
    field,
    middle_field,
    speed,
    warped,
    rows_in,
    cols_out,
    cols_in,
    vrows_in,
    vcols_out,
    vcols_in,
    weight,
    sums,
    pair_in,
    half,
    parts_in,
    denom_in,
    whole,
    load,
    z_send,
    z_recv,
    y_send,
    y_recv,
    step_send,
    step_recv,
    v_send,
    v_recv,
    pair_send,
    pair_recv,
    part_send,
    part_recv,
    denom_send,
    denom_recv,
    gather_send,
    gather_recv,
):
    subj = lax.axis_index("subj")
    space = lax.axis_index("space")
    row, col = space // TGY, space % TGY
    chip, core = subj // 2, subj % 2
    place = (
        (subj, ((row + 3) % 4) * TGY + col),
        (subj, ((row + 1) % 4) * TGY + col),
        (subj, row * TGY + (col + 3) % 4),
        (subj, row * TGY + (col + 1) % 4),
    )
    owners = [((chip + b // 2 + 1) % 8, core if b % 2 == 0 else 1 - core) for b in range(14)]
    owners.append((chip, 1 - core))
    peers = [(chip_at * 2 + core_at, space) for chip_at, core_at in owners]

    barrier = pltpu.get_barrier_semaphore()
    for device in list(place) + peers:
        pl.semaphore_signal(barrier, inc=1, device_id=device, device_id_type=MESH)
    loads = [pltpu.make_async_copy(moment_hbm.at[c], moment_ref.at[c], load.at[c]) for c in range(6)]
    loads.append(pltpu.make_async_copy(image_hbm, image_ref, load.at[6]))
    for copy in loads:
        copy.start()

    has = tuple(
        jnp.where(flag, 1.0, 0.0).astype(jnp.float32)
        for flag in (row > 0, row < 3, col > 0, col < TGY - 1)
    )
    lane = lax.broadcasted_iota(jnp.int32, (8, CZ), 1)
    tiles = [(PAD + 8 * t, 8 * t) for t in range(CY // 8)]

    def remote(src, dst, send, recv, device):
        return pltpu.make_async_remote_copy(
            src_ref=src,
            dst_ref=dst,
            send_sem=send,
            recv_sem=recv,
            device_id=device,
            device_id_type=MESH,
        )

    def loop(body, count, unroll=1):
        def step(i, carry):
            body(i)
            return carry

        lax.fori_loop(0, count, step, 0, unroll=unroll)

    def stage_edges(c):
        def body(x):
            edge_out[c, 0, x] = moment_ref[c, x, 0:EDGE, :].astype(jnp.float32)
            edge_out[c, 1, x] = moment_ref[c, x, CY - EDGE : CY, :].astype(jnp.float32)

        loop(body, CX, 8)

    def stage_image(s):
        def body(x):
            value = image_ref[s, x].astype(jnp.float32)
            warped[s, 0, x + 1, OWN, :] = value
            cols_out[s, 0, 0, pl.ds(x, 1), :] = value[0:1]
            cols_out[s, 0, 1, pl.ds(x, 1), :] = value[CY - 1 : CY]

        loop(body, CX, 4)

    def stage_first(x):
        field[0, wide + x] = moment_ref[0, x].astype(jnp.float32)

    loads[0].wait()
    loop(stage_first, CX, 8)
    for c in range(1, 4):
        loads[c].wait()
        stage_edges(c)
    pl.semaphore_wait(barrier, 19)

    def start_edges(c):
        pair = (
            remote(edge_out.at[c, 0], edge_in.at[c, 1], y_send.at[c, 0], y_recv.at[c, 0], place[W]),
            remote(edge_out.at[c, 1], edge_in.at[c, 0], y_send.at[c, 1], y_recv.at[c, 1], place[E]),
        )
        for copy in pair:
            copy.start()
        return pair

    def start_rows(s, k):
        slot = k % 2
        copies = (
            remote(warped.at[s, slot, 1, OWN], rows_in.at[s, k, 1], step_send.at[s, k, N], step_recv.at[s, k, N], place[N]),
            remote(warped.at[s, slot, CX, OWN], rows_in.at[s, k, 0], step_send.at[s, k, S], step_recv.at[s, k, S], place[S]),
        )
        for copy in copies:
            copy.start()
        return copies

    def start_cols(s, k):
        copies = (
            remote(cols_out.at[s, k, 0], cols_in.at[s, k, 1], step_send.at[s, k, W], step_recv.at[s, k, W], place[W]),
            remote(cols_out.at[s, k, 1], cols_in.at[s, k, 0], step_send.at[s, k, E], step_recv.at[s, k, E], place[E]),
        )
        for copy in copies:
            copy.start()
        return copies

    def start_speed_rows(s):
        a = 3 * s
        copies = (
            remote(speed.at[a, 1, OWN], vrows_in.at[s, 1], v_send.at[s, N], v_recv.at[s, N], place[N]),
            remote(speed.at[a, CX, OWN], vrows_in.at[s, 0], v_send.at[s, S], v_recv.at[s, S], place[S]),
        )
        for copy in copies:
            copy.start()
        return copies

    def start_speed_cols(s):
        copies = (
            remote(vcols_out.at[s, 0], vcols_in.at[s, 1], v_send.at[s, W], v_recv.at[s, W], place[W]),
            remote(vcols_out.at[s, 1], vcols_in.at[s, 0], v_send.at[s, E], v_recv.at[s, E], place[E]),
        )
        for copy in copies:
            copy.start()
        return copies

    def start_bulk(c):
        copies = (
            remote(field.at[c, pl.ds(wide, wide)], field.at[c, pl.ds(wide + CX, wide)], z_send.at[c, 0], z_recv.at[c, 0], place[N]),
            remote(field.at[c, pl.ds(CX, wide)], field.at[c, pl.ds(0, wide)], z_send.at[c, 1], z_recv.at[c, 1], place[S]),
        )
        for copy in copies:
            copy.start()
        return copies

    def start_middle():
        copies = (
            remote(middle_field.at[:, 0:EDGE], edge_in.at[0, 1], y_send.at[0, 0], y_recv.at[0, 0], place[W]),
            remote(middle_field.at[:, CY - EDGE : CY], edge_in.at[0, 0], y_send.at[0, 1], y_recv.at[0, 1], place[E]),
        )
        for copy in copies:
            copy.start()
        return copies

    edges = {1: start_edges(1)}
    bulk = {0: start_bulk(0)}
    for c in range(2, 4):
        edges[c] = start_edges(c)
    for c in range(4, 6):
        loads[c].wait()
        stage_edges(c)
    loads[6].wait()
    for s in range(2):
        stage_image(s)

    width = [widths_ref[a].astype(jnp.float32) for a in range(3)]
    out_id = lax.broadcasted_iota(jnp.int32, (CY, CY + 2 * EDGE), 0)
    in_id = lax.broadcasted_iota(jnp.int32, (CY, CY + 2 * EDGE), 1)
    dist = jnp.abs(in_id - EDGE - out_id).astype(jnp.float32)
    second = jnp.maximum(width[1] + 1.0 - dist, 0.0)
    second = jnp.where(in_id < EDGE, second * has[W], second)
    second = jnp.where(in_id >= EDGE + CY, second * has[E], second)
    second = second.astype(jnp.bfloat16)
    out_id = lax.broadcasted_iota(jnp.int32, (CZ, CZ), 0)
    in_id = lax.broadcasted_iota(jnp.int32, (CZ, CZ), 1)
    dist = jnp.abs(in_id - out_id).astype(jnp.float32)
    third = jnp.maximum(width[2] + 1.0 - dist, 0.0).astype(jnp.bfloat16)
    norm = 1.0
    for a in range(3):
        norm = norm * ((width[a] + 1.0) * (width[a] + 1.0))
    scale = jnp.full((8, CZ), 1.0 / STEPS, jnp.float32) / jnp.full((8, CZ), 1.0, jnp.float32) / norm

    def smooth_inner(c):
        group = 12 if c == 1 else 4

        def body(g):
            blocks = []
            for j in range(group):
                x = g * group + j
                ext = jnp.concatenate(
                    [
                        edge_in[c, 0, x].astype(jnp.bfloat16),
                        moment_ref[c, x],
                        edge_in[c, 1, x].astype(jnp.bfloat16),
                    ],
                    axis=0,
                )
                blocks.append(jnp.dot(second, ext, preferred_element_type=jnp.float32))
            value = jnp.concatenate(blocks, axis=0)
            high = value.astype(jnp.bfloat16)
            low = (value - high.astype(jnp.float32)).astype(jnp.bfloat16)
            value = jnp.dot(high, third, preferred_element_type=jnp.float32) + jnp.dot(
                low, third, preferred_element_type=jnp.float32
            )
            for j in range(group):
                field[c, wide + g * group + j] = value[j * CY : (j + 1) * CY]

        loop(body, CX // group)

    def split(value):
        high = value.astype(jnp.bfloat16)
        return high, (value - high.astype(jnp.float32)).astype(jnp.bfloat16)

    def smooth_inner_last():
        group = 4

        def body(g):
            blocks = []
            for j in range(group):
                x = g * group + j
                ext = jnp.concatenate([edge_in[0, 0, x], middle_field[x], edge_in[0, 1, x]], axis=0)
                blocks.append(
                    sum(jnp.dot(second, part, preferred_element_type=jnp.float32) for part in split(ext))
                )
            value = jnp.concatenate(blocks, axis=0)
            value = sum(jnp.dot(part, third, preferred_element_type=jnp.float32) for part in split(value))
            for j in range(group):
                speed[0, g * group + j + 1, OWN, :] = value[j * CY : (j + 1) * CY] * scale[0:1]

        loop(body, CX // group)

    def smooth_first(c):
        s, a = c // 3, c % 3

        def at(i, t, side=None):
            value = field[c, i, t : t + 8, :]
            return value if side is None else value * has[side]

        total, slope = [], []
        for _, t in tiles:
            sides = [N] * wide + [None] * CX
            first = [at(i, t, sides[i]) for i in range(2 * wide + 2)]
            total.append(sum((wide + 1.0 - abs(i - wide)) * first[i] for i in range(2 * wide + 1)))
            slope.append(sum(first[wide + 1 : 2 * wide + 2]) - sum(first[0 : wide + 1]))

        def emit(x, values):
            for (p, t), value in zip(tiles, values):
                if c == 0:
                    middle_field[x, t : t + 8, :] = value
                else:
                    speed[c, x + 1, p : p + 8, :] = value * scale
            if a == 1:
                vcols_out[s, 0, pl.ds(x, 1), :] = (values[0] * scale)[0:1]
                vcols_out[s, 1, pl.ds(x, 1), :] = (values[-1] * scale)[7:8]

        def advance(low, high):
            def step(i, carry):
                total, slope = carry
                emit(i, total)
                total = [p + q for p, q in zip(total, slope)]
                ahead = jnp.where(i + 2 * wide + 2 >= wide + CX, has[S], 1.0)
                behind = jnp.where(i < wide, has[N], 1.0)
                slope = [
                    q + (at(i + 2 * wide + 2, t) * ahead + at(i, t) * behind - 2.0 * at(i + wide + 1, t))
                    for q, (_, t) in zip(slope, tiles)
                ]
                return total, slope

            return lambda carry: lax.fori_loop(low, high, step, carry, unroll=2)

        total, slope = advance(0, CX - 2)((total, slope))
        emit(CX - 2, total)
        emit(CX - 1, [p + q for p, q in zip(total, slope)])

    def side_columns(target, columns, x):
        target[x + 1, PAD - 1 : PAD, :] = columns[0, pl.ds(x, 1), :] * has[W]
        target[x + 1, PAD + CY : PAD + CY + 1, :] = columns[1, pl.ds(x, 1), :] * has[E]

    def side_rows(target, rows):
        target[0, OWN, :] = rows[0] * has[N]
        target[CX + 1, OWN, :] = rows[1] * has[S]

    def transport(s, k, after, blocks=None):
        held, made = warped.at[s, k % 2], warped.at[s, (k + 1) % 2]
        side_rows(held, rows_in.at[s, k])

        def body(x):
            side_columns(held, cols_in.at[s, k], x)
            values = []
            for p, _ in tiles:
                centre = held[x + 1, p : p + 8, :]
                below = jnp.where(lane == 0, 0.0, pltpu.roll(centre, 1, 1))
                above = jnp.where(lane == CZ - 1, 0.0, pltpu.roll(centre, CZ - 1, 1))
                sides = (
                    (held[x, p : p + 8, :], held[x + 2, p : p + 8, :]),
                    (held[x + 1, p - 1 : p + 7, :], held[x + 1, p + 1 : p + 9, :]),
                    (below, above),
                )
                value = centre
                for a in range(3):
                    rate = speed[3 * s + a, x + 1, p : p + 8, :]
                    lower, upper = sides[a]
                    value = value - jnp.abs(rate) * (centre - jnp.where(rate > 0.0, lower, upper))
                made[x + 1, p : p + 8, :] = value
                values.append(value)
            after(x, values)

        if blocks is None and k < 3:
            body(0)
            body(CX - 1)
            copies = start_rows(s, k + 1)
            loop(lambda x: body(x + 1), CX - 2, 2 if s == 0 and k < 2 else 11)
            halos[s, k + 1] = copies + start_cols(s, k + 1)
        elif blocks is None:
            loop(body, CX, 8)
        else:
            for b, block in enumerate(blocks):
                loop(lambda r: body(3 * block + r), 3, 3)
                send_numer(b)

    def stage_columns(s, k):
        def after(x, values):
            cols_out[s, k, 0, pl.ds(x, 1), :] = values[0][0:1]
            cols_out[s, k, 1, pl.ds(x, 1), :] = values[-1][7:8]

        return after

    def wait(copies):
        for copy in copies:
            copy.wait()

    def weigh(s):
        first, middle, last = (speed.at[3 * s + a] for a in range(3))
        side_rows(first, vrows_in.at[s])
        flag = flags_ref[s].astype(jnp.float32)

        def body(x):
            side_columns(middle, vcols_in.at[s], x)
            for p, t in tiles:
                centre = last[x + 1, p : p + 8, :]
                below = jnp.where(lane == 0, 0.0, pltpu.roll(centre, 1, 1))
                above = jnp.where(lane == CZ - 1, 0.0, pltpu.roll(centre, CZ - 1, 1))
                total = first[x + 2, p : p + 8, :] - first[x, p : p + 8, :]
                total = total + (middle[x + 1, p + 1 : p + 9, :] - middle[x + 1, p - 1 : p + 7, :])
                total = total + (above - below)
                value = flag * jnp.exp(total * (0.5 * STEPS))
                weight[s, x, t : t + 8, :] = value
                if s == 0:
                    sums[1, x, t : t + 8, :] = value
                else:
                    sums[1, x, t : t + 8, :] += value

        loop(body, CX, 8)

    def piece(ref, chip_at, core_at):
        return ref.at[pl.ds(3 * chip_at, 3), pl.ds(pl.multiple_of(24 * core_at, 8), 24)]

    def send_numer(b):
        for k in (2 * b, 2 * b + 1):
            if k == 15:
                continue
            block = piece(sums.at[0], *owners[k])
            copy = remote(block, parts_in.at[k], part_send.at[k], part_recv.at[k], peers[k])
            copy.start()
            numer_parts.append(copy)

    numer_parts = []
    here = pl.multiple_of(24 * core, 8)
    there = pl.multiple_of(24 * (1 - core), 8)

    def start_pair():
        copy = remote(sums.at[1, :, pl.ds(there, 24)], pair_in, pair_send.at[0], pair_recv.at[0], peers[14])
        copy.start()
        return copy

    def add_pair():
        def body(x):
            half[x] = sums[1, x, pl.ds(here, 24), :] + pair_in[x]

        loop(body, CX, 8)

    def start_denom():
        copies = [
            remote(half.at[pl.ds(3 * owners[2 * b][0], 3)], denom_in.at[b], denom_send.at[b], denom_recv.at[b], peers[2 * b])
            for b in range(7)
        ]
        for copy in copies:
            copy.start()
        return copies

    halos = {}
    wait(edges[1])
    smooth_inner(1)
    bulk[1] = start_bulk(1)
    for s in range(2):
        halos[s, 0] = start_rows(s, 0) + start_cols(s, 0)
    wait(edges[2])
    smooth_inner(2)
    bulk[2] = start_bulk(2)
    wait(bulk[0])
    smooth_first(0)
    edges[0] = start_middle()
    edges[4] = start_edges(4)
    edges[5] = start_edges(5)
    wait(edges[3])
    smooth_inner(3)
    bulk[3] = start_bulk(3)
    wait(bulk[1])
    smooth_first(1)
    shift = {0: start_speed_cols(0)}
    wait(edges[0])
    smooth_inner_last()
    shift[0] += start_speed_rows(0)
    wait(edges[4])
    smooth_inner(4)
    bulk[4] = start_bulk(4)
    wait(edges[5])
    smooth_inner(5)
    wait(bulk[2])
    smooth_first(2)
    wait(halos[0, 0])
    transport(0, 0, stage_columns(0, 1))
    bulk[5] = start_bulk(5)
    wait(bulk[3])
    smooth_first(3)
    shift[1] = start_speed_rows(1)
    wait(shift[0])
    weigh(0)
    wait(halos[0, 1])
    transport(0, 1, stage_columns(0, 2))
    wait(bulk[4])
    smooth_first(4)
    shift[1] += start_speed_cols(1)
    wait(halos[1, 0])

    wait(bulk[5])
    smooth_first(5)
    transport(1, 0, stage_columns(1, 1))
    wait(halos[0, 2])
    transport(0, 2, stage_columns(0, 3))
    wait(shift[1])
    weigh(1)
    pair = start_pair()
    wait(halos[1, 1])
    transport(1, 1, stage_columns(1, 2))
    wait(halos[0, 3])
    transport(0, 3, lambda x, values: None)
    pair.wait()
    add_pair()
    wait(halos[1, 2])
    transport(1, 2, stage_columns(1, 3))
    denom_parts = start_denom()
    wait(halos[1, 3])

    def gather_sum(x, values):
        for (p, t), value in zip(tiles, values):
            sums[0, x, t : t + 8, :] = (
                weight[0, x, t : t + 8, :] * warped[0, 0, x + 1, p : p + 8, :] + weight[1, x, t : t + 8, :] * value
            )

    transport(1, 3, gather_sum, [owners[2 * b][0] for b in range(7)] + [chip])
    wait(denom_parts)
    denom = []
    for x in range(3):
        total = half[3 * chip + x]
        for k in range(7):
            total = total + denom_in[k, x]
        denom.append(1.0 + total)
    wait(numer_parts)
    for x in range(3):
        total = sums[0, 3 * chip + x, pl.ds(here, 24), :]
        for k in range(15):
            total = total + parts_in[k, x]
        whole[3 * chip + x, pl.ds(here, 24), :] = total / denom[x]

    own = piece(whole, chip, core)
    across = [remote(own, own, gather_send.at[b], gather_recv.at[b], peers[2 * b]) for b in range(7)]
    onward = [remote(own, own, gather_send.at[7], gather_recv.at[7], peers[14])]
    for copy in across + onward:
        copy.start()
    for b in range(7):
        across[b].wait_recv()
        block = piece(whole, (chip + 7 - b) % 8, core)
        onward.append(remote(block, block, gather_send.at[8 + b], gather_recv.at[8 + b], peers[14]))
        onward[-1].start()
    for copy in across:
        copy.wait_send()
    wait(onward)

    def finish(x):
        value = whole[x]
        template_ref[x] = value
        for s in range(2):
            mismatch_ref[s, x] = (warped[s, 0, x + 1, OWN, :] - value).astype(jnp.bfloat16)

    loop(finish, CX, 8)


def build(index, wide):
    f32 = jnp.float32
    dma = pltpu.SemaphoreType.DMA
    return pl.pallas_call(
        functools.partial(kernel, wide),
        out_shape=(
            jax.ShapeDtypeStruct((2, CX, CY, CZ), jnp.bfloat16),
            jax.ShapeDtypeStruct((CX, CY, CZ), f32),
        ),
        in_specs=[pl.BlockSpec(memory_space=pltpu.SMEM)] * 2 + [pl.BlockSpec(memory_space=pl.ANY)] * 2,
        out_specs=(pl.BlockSpec(memory_space=pltpu.VMEM),) * 2,
        scratch_shapes=[
            pltpu.VMEM((2, CX, CY, CZ), jnp.bfloat16),
            pltpu.VMEM((6, CX, CY, CZ), jnp.bfloat16),
            pltpu.VMEM((6, 2, CX, EDGE, CZ), f32),
            pltpu.VMEM((6, 2, CX, EDGE, CZ), f32),
            pltpu.VMEM((6, CX + 2 * wide, CY, CZ), f32),
            pltpu.VMEM((CX, CY, CZ), f32),
            pltpu.VMEM((6, CX + 2, CY + 2 * PAD, CZ), f32),
            pltpu.VMEM((2, 2, CX + 2, CY + 2 * PAD, CZ), f32),
            pltpu.VMEM((2, 4, 2, CY, CZ), f32),
            pltpu.VMEM((2, 4, 2, CX, CZ), f32),
            pltpu.VMEM((2, 4, 2, CX, CZ), f32),
            pltpu.VMEM((2, 2, CY, CZ), f32),
            pltpu.VMEM((2, 2, CX, CZ), f32),
            pltpu.VMEM((2, 2, CX, CZ), f32),
            pltpu.VMEM((2, CX, CY, CZ), f32),
            pltpu.VMEM((2, CX, CY, CZ), f32),
            pltpu.VMEM((CX, 24, CZ), f32),
            pltpu.VMEM((CX, 24, CZ), f32),
            pltpu.VMEM((15, 3, 24, CZ), f32),
            pltpu.VMEM((7, 3, 24, CZ), f32),
            pltpu.VMEM((CX, CY, CZ), f32),
            dma((7,)),
            dma((6, 2)),
            dma((6, 2)),
            dma((6, 2)),
            dma((6, 2)),
            dma((2, 4, 4)),
            dma((2, 4, 4)),
            dma((2, 4)),
            dma((2, 4)),
            dma((1,)),
            dma((1,)),
            dma((15,)),
            dma((15,)),
            dma((7,)),
            dma((7,)),
            dma((15,)),
            dma((15,)),
        ],
        compiler_params=pltpu.CompilerParams(
            collective_id=index, has_side_effects=True, vmem_limit_bytes=48 * 2**20
        ),
    )


def per_device(image, momentum, tissue_flags, band_widths):
    args = (
        band_widths,
        tissue_flags.reshape(2),
        image.reshape(2, CX, CY, CZ),
        momentum.reshape(6, CX, CY, CZ),
    )
    which = jnp.clip((band_widths[0] - 8) // 2, 0, 2)
    mismatch, template = lax.switch(which, [build(i, 8 + 2 * i) for i in range(3)], *args)
    return mismatch[:, None], template[None]


def solution(mesh):
    return jax.shard_map(
        per_device,
        mesh=mesh,
        in_specs=(
            P("subj", "space", None, None, None),
            P("subj", None, "space", None, None, None),
            P("subj", "space"),
            P(),
        ),
        out_specs=(P("subj", "space", None, None, None), P("space", None, None, None)),
        check_vma=False,
    )
```

```python
import functools

import jax
import jax.numpy as jnp
from jax import lax
from jax.experimental import pallas as pl
from jax.experimental.pallas import tpu as pltpu
from jax.sharding import PartitionSpec as P

TGY = 4
STEPS = 4
CX = 24
CY = 48
CZ = 128
EDGE = 16
PAD = 8
MESH = pl.DeviceIdType.MESH
OWN = slice(PAD, PAD + CY)
N, S, W, E = range(4)


def kernel(
    wide,
    widths_ref,
    flags_ref,
    image_hbm,
    moment_hbm,
    mismatch_ref,
    template_ref,
    image_ref,
    moment_ref,
    edge_out,
    edge_in,
    field,
    middle_field,
    speed,
    warped,
    rows_in,
    cols_out,
    cols_in,
    vrows_in,
    vcols_out,
    vcols_in,
    weight,
    sums,
    pair_in,
    half,
    parts_in,
    denom_in,
    whole,
    load,
    z_send,
    z_recv,
    y_send,
    y_recv,
    step_send,
    step_recv,
    v_send,
    v_recv,
    pair_send,
    pair_recv,
    part_send,
    part_recv,
    denom_send,
    denom_recv,
    gather_send,
    gather_recv,
):
    subj = lax.axis_index("subj")
    space = lax.axis_index("space")
    row, col = space // TGY, space % TGY
    chip, core = subj // 2, subj % 2
    place = (
        (subj, ((row + 3) % 4) * TGY + col),
        (subj, ((row + 1) % 4) * TGY + col),
        (subj, row * TGY + (col + 3) % 4),
        (subj, row * TGY + (col + 1) % 4),
    )
    layer, spot = chip // 4, chip % 4
    far = [(1, 2), (1, 1), (1, 3), (1, 0), (0, 2), (0, 1), (0, 3)]
    chips = [((layer + dz) % 2) * 4 + (spot + dx) % 4 for dz, dx in far]
    sources = [((layer + dz) % 2) * 4 + (spot + 4 - dx) % 4 for dz, dx in far]
    owners = [(chips[b // 2], core if b % 2 == 0 else 1 - core) for b in range(14)]
    owners.append((chip, 1 - core))
    peers = [(chip_at * 2 + core_at, space) for chip_at, core_at in owners]

    barrier = pltpu.get_barrier_semaphore()
    for device in list(place) + peers:
        pl.semaphore_signal(barrier, inc=1, device_id=device, device_id_type=MESH)
    loads = [pltpu.make_async_copy(moment_hbm.at[c], moment_ref.at[c], load.at[c]) for c in range(6)]
    loads.append(pltpu.make_async_copy(image_hbm, image_ref, load.at[6]))
    for copy in loads:
        copy.start()

    has = tuple(
        jnp.where(flag, 1.0, 0.0).astype(jnp.float32)
        for flag in (row > 0, row < 3, col > 0, col < TGY - 1)
    )
    lane = lax.broadcasted_iota(jnp.int32, (8, CZ), 1)
    tiles = [(PAD + 8 * t, 8 * t) for t in range(CY // 8)]

    def remote(src, dst, send, recv, device):
        return pltpu.make_async_remote_copy(
            src_ref=src,
            dst_ref=dst,
            send_sem=send,
            recv_sem=recv,
            device_id=device,
            device_id_type=MESH,
        )

    def loop(body, count, unroll=1):
        def step(i, carry):
            body(i)
            return carry

        lax.fori_loop(0, count, step, 0, unroll=unroll)

    def stage_edges(c):
        def body(x):
            edge_out[c, 0, x] = moment_ref[c, x, 0:EDGE, :].astype(jnp.float32)
            edge_out[c, 1, x] = moment_ref[c, x, CY - EDGE : CY, :].astype(jnp.float32)

        loop(body, CX, 8)

    def stage_image(s):
        def body(x):
            value = image_ref[s, x].astype(jnp.float32)
            warped[s, 0, x + 1, OWN, :] = value
            cols_out[s, 0, 0, pl.ds(x, 1), :] = value[0:1]
            cols_out[s, 0, 1, pl.ds(x, 1), :] = value[CY - 1 : CY]

        loop(body, CX, 4)

    def stage_first(x):
        field[0, wide + x] = moment_ref[0, x].astype(jnp.float32)

    loads[0].wait()
    loop(stage_first, CX, 8)
    for c in range(1, 4):
        loads[c].wait()
        stage_edges(c)
    pl.semaphore_wait(barrier, 19)

    def start_edges(c):
        pair = (
            remote(edge_out.at[c, 0], edge_in.at[c, 1], y_send.at[c, 0], y_recv.at[c, 0], place[W]),
            remote(edge_out.at[c, 1], edge_in.at[c, 0], y_send.at[c, 1], y_recv.at[c, 1], place[E]),
        )
        for copy in pair:
            copy.start()
        return pair

    def start_rows(s, k):
        slot = k % 2
        copies = (
            remote(warped.at[s, slot, 1, OWN], rows_in.at[s, k, 1], step_send.at[s, k, N], step_recv.at[s, k, N], place[N]),
            remote(warped.at[s, slot, CX, OWN], rows_in.at[s, k, 0], step_send.at[s, k, S], step_recv.at[s, k, S], place[S]),
        )
        for copy in copies:
            copy.start()
        return copies

    def start_cols(s, k):
        copies = (
            remote(cols_out.at[s, k, 0], cols_in.at[s, k, 1], step_send.at[s, k, W], step_recv.at[s, k, W], place[W]),
            remote(cols_out.at[s, k, 1], cols_in.at[s, k, 0], step_send.at[s, k, E], step_recv.at[s, k, E], place[E]),
        )
        for copy in copies:
            copy.start()
        return copies

    def start_speed_rows(s):
        a = 3 * s
        copies = (
            remote(speed.at[a, 1, OWN], vrows_in.at[s, 1], v_send.at[s, N], v_recv.at[s, N], place[N]),
            remote(speed.at[a, CX, OWN], vrows_in.at[s, 0], v_send.at[s, S], v_recv.at[s, S], place[S]),
        )
        for copy in copies:
            copy.start()
        return copies

    def start_speed_cols(s):
        copies = (
            remote(vcols_out.at[s, 0], vcols_in.at[s, 1], v_send.at[s, W], v_recv.at[s, W], place[W]),
            remote(vcols_out.at[s, 1], vcols_in.at[s, 0], v_send.at[s, E], v_recv.at[s, E], place[E]),
        )
        for copy in copies:
            copy.start()
        return copies

    def start_bulk(c):
        copies = (
            remote(field.at[c, pl.ds(wide, wide)], field.at[c, pl.ds(wide + CX, wide)], z_send.at[c, 0], z_recv.at[c, 0], place[N]),
            remote(field.at[c, pl.ds(CX, wide)], field.at[c, pl.ds(0, wide)], z_send.at[c, 1], z_recv.at[c, 1], place[S]),
        )
        for copy in copies:
            copy.start()
        return copies

    def start_middle():
        copies = (
            remote(middle_field.at[:, 0:EDGE], edge_in.at[0, 1], y_send.at[0, 0], y_recv.at[0, 0], place[W]),
            remote(middle_field.at[:, CY - EDGE : CY], edge_in.at[0, 0], y_send.at[0, 1], y_recv.at[0, 1], place[E]),
        )
        for copy in copies:
            copy.start()
        return copies

    edges = {1: start_edges(1)}
    bulk = {0: start_bulk(0)}
    for c in range(2, 4):
        edges[c] = start_edges(c)
    for c in range(4, 6):
        loads[c].wait()
        stage_edges(c)
    loads[6].wait()
    for s in range(2):
        stage_image(s)

    width = [widths_ref[a].astype(jnp.float32) for a in range(3)]
    out_id = lax.broadcasted_iota(jnp.int32, (CY, CY + 2 * EDGE), 0)
    in_id = lax.broadcasted_iota(jnp.int32, (CY, CY + 2 * EDGE), 1)
    dist = jnp.abs(in_id - EDGE - out_id).astype(jnp.float32)
    second = jnp.maximum(width[1] + 1.0 - dist, 0.0)
    second = jnp.where(in_id < EDGE, second * has[W], second)
    second = jnp.where(in_id >= EDGE + CY, second * has[E], second)
    second = second.astype(jnp.bfloat16)
    out_id = lax.broadcasted_iota(jnp.int32, (CZ, CZ), 0)
    in_id = lax.broadcasted_iota(jnp.int32, (CZ, CZ), 1)
    dist = jnp.abs(in_id - out_id).astype(jnp.float32)
    third = jnp.maximum(width[2] + 1.0 - dist, 0.0).astype(jnp.bfloat16)
    norm = 1.0
    for a in range(3):
        norm = norm * ((width[a] + 1.0) * (width[a] + 1.0))
    scale = jnp.full((8, CZ), 1.0 / STEPS, jnp.float32) / jnp.full((8, CZ), 1.0, jnp.float32) / norm

    def smooth_inner(c):
        group = 12 if c == 1 else 4

        def body(g):
            blocks = []
            for j in range(group):
                x = g * group + j
                ext = jnp.concatenate(
                    [
                        edge_in[c, 0, x].astype(jnp.bfloat16),
                        moment_ref[c, x],
                        edge_in[c, 1, x].astype(jnp.bfloat16),
                    ],
                    axis=0,
                )
                blocks.append(jnp.dot(second, ext, preferred_element_type=jnp.float32))
            value = jnp.concatenate(blocks, axis=0)
            high = value.astype(jnp.bfloat16)
            low = (value - high.astype(jnp.float32)).astype(jnp.bfloat16)
            value = jnp.dot(high, third, preferred_element_type=jnp.float32) + jnp.dot(
                low, third, preferred_element_type=jnp.float32
            )
            for j in range(group):
                field[c, wide + g * group + j] = value[j * CY : (j + 1) * CY]

        loop(body, CX // group)

    def split(value):
        high = value.astype(jnp.bfloat16)
        return high, (value - high.astype(jnp.float32)).astype(jnp.bfloat16)

    def smooth_inner_last():
        group = 4

        def body(g):
            blocks = []
            for j in range(group):
                x = g * group + j
                ext = jnp.concatenate([edge_in[0, 0, x], middle_field[x], edge_in[0, 1, x]], axis=0)
                blocks.append(
                    sum(jnp.dot(second, part, preferred_element_type=jnp.float32) for part in split(ext))
                )
            value = jnp.concatenate(blocks, axis=0)
            value = sum(jnp.dot(part, third, preferred_element_type=jnp.float32) for part in split(value))
            for j in range(group):
                speed[0, g * group + j + 1, OWN, :] = value[j * CY : (j + 1) * CY] * scale[0:1]

        loop(body, CX // group)

    def smooth_first(c):
        s, a = c // 3, c % 3

        def at(i, t, side=None):
            value = field[c, i, t : t + 8, :]
            return value if side is None else value * has[side]

        total, slope = [], []
        for _, t in tiles:
            sides = [N] * wide + [None] * CX
            first = [at(i, t, sides[i]) for i in range(2 * wide + 2)]
            total.append(sum((wide + 1.0 - abs(i - wide)) * first[i] for i in range(2 * wide + 1)))
            slope.append(sum(first[wide + 1 : 2 * wide + 2]) - sum(first[0 : wide + 1]))

        def emit(x, values):
            for (p, t), value in zip(tiles, values):
                if c == 0:
                    middle_field[x, t : t + 8, :] = value
                else:
                    speed[c, x + 1, p : p + 8, :] = value * scale
            if a == 1:
                vcols_out[s, 0, pl.ds(x, 1), :] = (values[0] * scale)[0:1]
                vcols_out[s, 1, pl.ds(x, 1), :] = (values[-1] * scale)[7:8]

        def advance(low, high):
            def step(i, carry):
                total, slope = carry
                emit(i, total)
                total = [p + q for p, q in zip(total, slope)]
                ahead = jnp.where(i + 2 * wide + 2 >= wide + CX, has[S], 1.0)
                behind = jnp.where(i < wide, has[N], 1.0)
                slope = [
                    q + (at(i + 2 * wide + 2, t) * ahead + at(i, t) * behind - 2.0 * at(i + wide + 1, t))
                    for q, (_, t) in zip(slope, tiles)
                ]
                return total, slope

            return lambda carry: lax.fori_loop(low, high, step, carry, unroll=2)

        total, slope = advance(0, CX - 2)((total, slope))
        emit(CX - 2, total)
        emit(CX - 1, [p + q for p, q in zip(total, slope)])

    def side_columns(target, columns, x):
        target[x + 1, PAD - 1 : PAD, :] = columns[0, pl.ds(x, 1), :] * has[W]
        target[x + 1, PAD + CY : PAD + CY + 1, :] = columns[1, pl.ds(x, 1), :] * has[E]

    def side_rows(target, rows):
        target[0, OWN, :] = rows[0] * has[N]
        target[CX + 1, OWN, :] = rows[1] * has[S]

    def transport(s, k, after, blocks=None):
        held, made = warped.at[s, k % 2], warped.at[s, (k + 1) % 2]
        side_rows(held, rows_in.at[s, k])

        def body(x):
            side_columns(held, cols_in.at[s, k], x)
            values = []
            for p, _ in tiles:
                centre = held[x + 1, p : p + 8, :]
                below = jnp.where(lane == 0, 0.0, pltpu.roll(centre, 1, 1))
                above = jnp.where(lane == CZ - 1, 0.0, pltpu.roll(centre, CZ - 1, 1))
                sides = (
                    (held[x, p : p + 8, :], held[x + 2, p : p + 8, :]),
                    (held[x + 1, p - 1 : p + 7, :], held[x + 1, p + 1 : p + 9, :]),
                    (below, above),
                )
                value = centre
                for a in range(3):
                    rate = speed[3 * s + a, x + 1, p : p + 8, :]
                    lower, upper = sides[a]
                    value = value - jnp.abs(rate) * (centre - jnp.where(rate > 0.0, lower, upper))
                made[x + 1, p : p + 8, :] = value
                values.append(value)
            after(x, values)

        if blocks is None and k < 3:
            body(0)
            body(CX - 1)
            copies = start_rows(s, k + 1)
            loop(lambda x: body(x + 1), CX - 2, 2 if s == 0 and k < 2 else 11)
            halos[s, k + 1] = copies + start_cols(s, k + 1)
        elif blocks is None:
            loop(body, CX, 8)
        else:
            for b, block in enumerate(blocks):
                loop(lambda r: body(3 * block + r), 3, 3)
                send_numer(b)

    def stage_columns(s, k):
        def after(x, values):
            cols_out[s, k, 0, pl.ds(x, 1), :] = values[0][0:1]
            cols_out[s, k, 1, pl.ds(x, 1), :] = values[-1][7:8]

        return after

    def wait(copies):
        for copy in copies:
            copy.wait()

    def weigh(s):
        first, middle, last = (speed.at[3 * s + a] for a in range(3))
        side_rows(first, vrows_in.at[s])
        flag = flags_ref[s].astype(jnp.float32)

        def body(x):
            side_columns(middle, vcols_in.at[s], x)
            for p, t in tiles:
                centre = last[x + 1, p : p + 8, :]
                below = jnp.where(lane == 0, 0.0, pltpu.roll(centre, 1, 1))
                above = jnp.where(lane == CZ - 1, 0.0, pltpu.roll(centre, CZ - 1, 1))
                total = first[x + 2, p : p + 8, :] - first[x, p : p + 8, :]
                total = total + (middle[x + 1, p + 1 : p + 9, :] - middle[x + 1, p - 1 : p + 7, :])
                total = total + (above - below)
                value = flag * jnp.exp(total * (0.5 * STEPS))
                weight[s, x, t : t + 8, :] = value
                if s == 0:
                    sums[1, x, t : t + 8, :] = value
                else:
                    sums[1, x, t : t + 8, :] += value

        loop(body, CX, 8)

    def piece(ref, chip_at, core_at):
        return ref.at[pl.ds(3 * chip_at, 3), pl.ds(pl.multiple_of(24 * core_at, 8), 24)]

    def send_numer(b):
        for k in (2 * b, 2 * b + 1):
            if k == 15:
                continue
            block = piece(sums.at[0], *owners[k])
            copy = remote(block, parts_in.at[k], part_send.at[k], part_recv.at[k], peers[k])
            copy.start()
            numer_parts.append(copy)

    numer_parts = []
    here = pl.multiple_of(24 * core, 8)
    there = pl.multiple_of(24 * (1 - core), 8)

    def start_pair():
        copy = remote(sums.at[1, :, pl.ds(there, 24)], pair_in, pair_send.at[0], pair_recv.at[0], peers[14])
        copy.start()
        return copy

    def add_pair():
        def body(x):
            half[x] = sums[1, x, pl.ds(here, 24), :] + pair_in[x]

        loop(body, CX, 8)

    def start_denom():
        copies = [
            remote(half.at[pl.ds(3 * owners[2 * b][0], 3)], denom_in.at[b], denom_send.at[b], denom_recv.at[b], peers[2 * b])
            for b in range(7)
        ]
        for copy in copies:
            copy.start()
        return copies

    halos = {}
    wait(edges[1])
    smooth_inner(1)
    bulk[1] = start_bulk(1)
    for s in range(2):
        halos[s, 0] = start_rows(s, 0) + start_cols(s, 0)
    wait(edges[2])
    smooth_inner(2)
    bulk[2] = start_bulk(2)
    wait(bulk[0])
    smooth_first(0)
    edges[0] = start_middle()
    edges[4] = start_edges(4)
    edges[5] = start_edges(5)
    wait(edges[3])
    smooth_inner(3)
    bulk[3] = start_bulk(3)
    wait(bulk[1])
    smooth_first(1)
    shift = {0: start_speed_cols(0)}
    wait(edges[0])
    smooth_inner_last()
    shift[0] += start_speed_rows(0)
    wait(edges[4])
    smooth_inner(4)
    bulk[4] = start_bulk(4)
    wait(edges[5])
    smooth_inner(5)
    wait(bulk[2])
    smooth_first(2)
    wait(halos[0, 0])
    transport(0, 0, stage_columns(0, 1))
    bulk[5] = start_bulk(5)
    wait(bulk[3])
    smooth_first(3)
    shift[1] = start_speed_rows(1)
    wait(shift[0])
    weigh(0)
    wait(halos[0, 1])
    transport(0, 1, stage_columns(0, 2))
    wait(bulk[4])
    smooth_first(4)
    shift[1] += start_speed_cols(1)
    wait(halos[1, 0])

    wait(bulk[5])
    smooth_first(5)
    transport(1, 0, stage_columns(1, 1))
    wait(halos[0, 2])
    transport(0, 2, stage_columns(0, 3))
    wait(shift[1])
    weigh(1)
    pair = start_pair()
    wait(halos[1, 1])
    transport(1, 1, stage_columns(1, 2))
    wait(halos[0, 3])
    transport(0, 3, lambda x, values: None)
    pair.wait()
    add_pair()
    wait(halos[1, 2])
    transport(1, 2, stage_columns(1, 3))
    denom_parts = start_denom()
    wait(halos[1, 3])

    def gather_sum(x, values):
        for (p, t), value in zip(tiles, values):
            sums[0, x, t : t + 8, :] = (
                weight[0, x, t : t + 8, :] * warped[0, 0, x + 1, p : p + 8, :] + weight[1, x, t : t + 8, :] * value
            )

    transport(1, 3, gather_sum, [owners[2 * b][0] for b in range(7)] + [chip])
    wait(denom_parts)
    denom = []
    for x in range(3):
        total = half[3 * chip + x]
        for k in range(7):
            total = total + denom_in[k, x]
        denom.append(1.0 + total)
    wait(numer_parts)
    for x in range(3):
        total = sums[0, 3 * chip + x, pl.ds(here, 24), :]
        for k in range(15):
            total = total + parts_in[k, x]
        whole[3 * chip + x, pl.ds(here, 24), :] = total / denom[x]

    own = piece(whole, chip, core)
    across = [remote(own, own, gather_send.at[b], gather_recv.at[b], peers[2 * b]) for b in range(7)]
    onward = [remote(own, own, gather_send.at[7], gather_recv.at[7], peers[14])]
    for copy in across + onward:
        copy.start()
    for b in range(7):
        across[b].wait_recv()
        block = piece(whole, sources[b], core)
        onward.append(remote(block, block, gather_send.at[8 + b], gather_recv.at[8 + b], peers[14]))
        onward[-1].start()
    for copy in across:
        copy.wait_send()
    wait(onward)

    def finish(x):
        value = whole[x]
        template_ref[x] = value
        for s in range(2):
            mismatch_ref[s, x] = (warped[s, 0, x + 1, OWN, :] - value).astype(jnp.bfloat16)

    loop(finish, CX, 8)


def build(index, wide):
    f32 = jnp.float32
    dma = pltpu.SemaphoreType.DMA
    return pl.pallas_call(
        functools.partial(kernel, wide),
        out_shape=(
            jax.ShapeDtypeStruct((2, CX, CY, CZ), jnp.bfloat16),
            jax.ShapeDtypeStruct((CX, CY, CZ), f32),
        ),
        in_specs=[pl.BlockSpec(memory_space=pltpu.SMEM)] * 2 + [pl.BlockSpec(memory_space=pl.ANY)] * 2,
        out_specs=(pl.BlockSpec(memory_space=pltpu.VMEM),) * 2,
        scratch_shapes=[
            pltpu.VMEM((2, CX, CY, CZ), jnp.bfloat16),
            pltpu.VMEM((6, CX, CY, CZ), jnp.bfloat16),
            pltpu.VMEM((6, 2, CX, EDGE, CZ), f32),
            pltpu.VMEM((6, 2, CX, EDGE, CZ), f32),
            pltpu.VMEM((6, CX + 2 * wide, CY, CZ), f32),
            pltpu.VMEM((CX, CY, CZ), f32),
            pltpu.VMEM((6, CX + 2, CY + 2 * PAD, CZ), f32),
            pltpu.VMEM((2, 2, CX + 2, CY + 2 * PAD, CZ), f32),
            pltpu.VMEM((2, 4, 2, CY, CZ), f32),
            pltpu.VMEM((2, 4, 2, CX, CZ), f32),
            pltpu.VMEM((2, 4, 2, CX, CZ), f32),
            pltpu.VMEM((2, 2, CY, CZ), f32),
            pltpu.VMEM((2, 2, CX, CZ), f32),
            pltpu.VMEM((2, 2, CX, CZ), f32),
            pltpu.VMEM((2, CX, CY, CZ), f32),
            pltpu.VMEM((2, CX, CY, CZ), f32),
            pltpu.VMEM((CX, 24, CZ), f32),
            pltpu.VMEM((CX, 24, CZ), f32),
            pltpu.VMEM((15, 3, 24, CZ), f32),
            pltpu.VMEM((7, 3, 24, CZ), f32),
            pltpu.VMEM((CX, CY, CZ), f32),
            dma((7,)),
            dma((6, 2)),
            dma((6, 2)),
            dma((6, 2)),
            dma((6, 2)),
            dma((2, 4, 4)),
            dma((2, 4, 4)),
            dma((2, 4)),
            dma((2, 4)),
            dma((1,)),
            dma((1,)),
            dma((15,)),
            dma((15,)),
            dma((7,)),
            dma((7,)),
            dma((15,)),
            dma((15,)),
        ],
        compiler_params=pltpu.CompilerParams(
            collective_id=index, has_side_effects=True, vmem_limit_bytes=48 * 2**20
        ),
    )


def per_device(image, momentum, tissue_flags, band_widths):
    args = (
        band_widths,
        tissue_flags.reshape(2),
        image.reshape(2, CX, CY, CZ),
        momentum.reshape(6, CX, CY, CZ),
    )
    which = jnp.clip((band_widths[0] - 8) // 2, 0, 2)
    mismatch, template = lax.switch(which, [build(i, 8 + 2 * i) for i in range(3)], *args)
    return mismatch[:, None], template[None]


def solution(mesh):
    return jax.shard_map(
        per_device,
        mesh=mesh,
        in_specs=(
            P("subj", "space", None, None, None),
            P("subj", None, "space", None, None, None),
            P("subj", "space"),
            P(),
        ),
        out_specs=(P("subj", "space", None, None, None), P("space", None, None, None)),
        check_vma=False,
    )
```
